32 devices in a mesh: seq: 8 (over z, x), head: 4 (over y, core).
Axes of the slice: x: 2, y: 2, z: 4, core: 2. Of those that a mesh axis runs over, the one named last changes fastest.
Arguments:
- queries: bfloat16 [4096, 512], P('seq', 'head'), may hold values from -6 to 6
- key_vectors: bfloat16 [4096, 512], P('seq', 'head'), may hold values from -6 to 6
- value_vectors: bfloat16 [4096, 512], P('seq', 'head'), may hold values from -6 to 6
- attn_out: bfloat16 [4096, 512], P('seq', 'head'), may hold values from -6 to 6
- out_grad: bfloat16 [4096, 512], P('seq', 'head'), may hold values from -6 to 6
- log_norm: float32 [8, 4096], P('head', 'seq'), may hold values from 5 to 7
- doc_offsets: int32 [17], replicated, may hold values from 0 to 4096, as said below
Outputs:
- grad_queries: bfloat16 [4096, 512], P(('seq', 'head'))
- grad_keys: bfloat16 [4096, 512], P(('seq', 'head'))
- grad_values: bfloat16 [4096, 512], P(('seq', 'head'))
The draws below stay inside these ranges and needn't reach their ends.
Inputs may be any that keep to these rules, and one draw needn't show every extreme that they name: doc_offsets[0] is 0 and doc_offsets[16] is 4096; the offsets never fall; document k holds tokens doc_offsets[k] to doc_offsets[k + 1] - 1 and may be empty; no document holds more than 1024 tokens and one holds exactly 1024.
All inputs are finite; a program needn't handle non-finite values.
Results may differ from the reference program's by a relative error of at most 0.0052.
Values may be sent and summed in bfloat16 or wider, within the bound.
A program may use at most 64 MiB of HBM per device.

```python
import jax
import jax.numpy as jnp
from jax import lax

HEADS = 8
HD = 64
TOK_DEV = 512
TOKENS = 4096
SPAN = 2
DOCMAX = 1024
DOCMIN = 256
NDOC = 16
N_SEQ = 8


def draw_doc_offsets(key, part):
    key = jax.random.fold_in(key, 7)
    first_key, second_key = jax.random.split(key)
    lengths = jax.random.randint(first_key, (NDOC,), DOCMIN, DOCMAX + 1, dtype=jnp.int32)
    longest = jax.random.randint(second_key, (), 0, TOKENS // DOCMAX, dtype=jnp.int32)
    lengths = jnp.where(jnp.arange(NDOC, dtype=jnp.int32) == longest, DOCMAX, lengths)
    doc_ends = jnp.minimum(jnp.cumsum(lengths), TOKENS).astype(jnp.int32)
    return jnp.concatenate([jnp.zeros((1,), jnp.int32), doc_ends])


def block_levels(own_key, extent, pieces, smallest, largest):
    gain, own = 1.0, jax.random.fold_in(own_key, 6)
    for dim, shards_of in pieces:
        steps = jnp.exp(jax.random.uniform(jax.random.fold_in(own, dim), (shards_of,), jnp.float32, smallest / len(pieces), largest / len(pieces)))
        gain = gain * jnp.repeat(steps, extent[dim] // shards_of).reshape([-1 if axis == dim else 1 for axis in range(len(extent))])
    return gain


def noise(stream_key, dims, deviation, limit, cuts=(), kind=jnp.bfloat16):
    entries = jax.random.normal(stream_key, dims, jnp.float32) * deviation
    if len(cuts) > 0:
        entries = block_levels(stream_key, dims, cuts, -0.22, 0.18) * entries
    return jnp.clip(entries, min=-limit, max=limit).astype(kind)


def setup_inputs(seed: int = 0) -> dict:
    splits = jax.random.split(jax.random.key(seed), 8)
    queries = noise(splits[0], (TOKENS, HEADS * HD), 1.0, 6.0, ((0, 8), (1, 4)))
    key_vectors = noise(splits[1], (TOKENS, HEADS * HD), 1.0, 6.0, ((0, 8), (1, 4)))
    value_vectors = noise(splits[2], (TOKENS, HEADS * HD), 1.0, 6.0, ((0, 8), (1, 4)))
    attn_out = noise(splits[3], (TOKENS, HEADS * HD), 1.0, 6.0, ((0, 8), (1, 4)))
    out_grad = noise(splits[4], (TOKENS, HEADS * HD), 1.0, 6.0, ((0, 8), (1, 4)))
    log_norm = jnp.clip(5.0 + 2.0 * jax.random.uniform(splits[5], (HEADS, TOKENS), jnp.float32) ** block_levels(splits[5], (HEADS, TOKENS), ((0, 4), (1, 8)), -0.2, 0.2), 5.0, 7.0)
    doc_offsets = draw_doc_offsets(jax.random.fold_in(splits[7], 71), 0)
    return {"queries": queries, "key_vectors": key_vectors, "value_vectors": value_vectors, "attn_out": attn_out, "out_grad": out_grad, "log_norm": log_norm, "doc_offsets": doc_offsets}


def doc_index(doc_offsets, first, count):
    positions = first + jnp.arange(count, dtype=jnp.int32)
    return jnp.sum((doc_offsets[1:, None] <= positions[None, :]).astype(jnp.int32), axis=0)


def head_delta(out_grad, attn_out, head_count, head_width):
    product = out_grad.astype(jnp.float32) * attn_out.astype(jnp.float32)
    return jnp.sum(product.reshape(product.shape[0], head_count, head_width), axis=2).T


def contract_last(left, right):
    return lax.dot_general(left, right, (((1,), (1,)), ((), ())), preferred_element_type=jnp.float32)


def contract_first(left, right):
    return lax.dot_general(left, right, (((0,), (0,)), ((), ())), preferred_element_type=jnp.float32)


def pair_terms(query_part, grad_part, norm_part, delta_part, query_docs, key_part, value_part, key_docs, head_count, head_width):
    score_scale = head_width ** -0.5
    same_doc = query_docs[:, None] == key_docs[None, :]
    query_grads, key_grads, value_grads = [], [], []
    for head_index in range(head_count):
        low = head_index * head_width
        query_head = query_part[:, low:low + head_width]
        grad_head = grad_part[:, low:low + head_width]
        key_head = key_part[:, low:low + head_width]
        value_head = value_part[:, low:low + head_width]
        scores = contract_last(query_head, key_head)
        prob_full = jnp.where(same_doc, jnp.exp(scores * score_scale - norm_part[head_index][:, None]), jnp.float32(0.0))
        prob_half = prob_full.astype(jnp.bfloat16)
        grad_probs = contract_last(grad_head, value_head)
        grad_scores = (prob_full * (grad_probs - delta_part[head_index][:, None])).astype(jnp.bfloat16)
        query_grads.append(score_scale * jnp.dot(grad_scores, key_head, preferred_element_type=jnp.float32))
        key_grads.append(score_scale * contract_first(grad_scores, query_head))
        value_grads.append(contract_first(prob_half, grad_head))
    return (jnp.concatenate(query_grads, axis=1), jnp.concatenate(key_grads, axis=1), jnp.concatenate(value_grads, axis=1))


def reference(queries, key_vectors, value_vectors, attn_out, out_grad, log_norm, doc_offsets):
    block_count = N_SEQ
    feat_count = HEADS * HD
    all_docs = doc_index(doc_offsets, 0, TOKENS)
    all_delta = head_delta(out_grad, attn_out, HEADS, HD)

    def visit_block(totals, block_index):
        key_total, value_total = totals
        query_start = block_index * TOK_DEV
        query_part = lax.dynamic_slice_in_dim(queries, query_start, TOK_DEV, 0)
        grad_part = lax.dynamic_slice_in_dim(out_grad, query_start, TOK_DEV, 0)
        norm_part = lax.dynamic_slice_in_dim(log_norm, query_start, TOK_DEV, 1)
        delta_part = lax.dynamic_slice_in_dim(all_delta, query_start, TOK_DEV, 1)
        query_docs = lax.dynamic_slice_in_dim(all_docs, query_start, TOK_DEV, 0)
        query_total = jnp.zeros((TOK_DEV, feat_count), jnp.float32)
        for offset_blocks in range(-SPAN, SPAN + 1):
            key_block = block_index + offset_blocks
            in_range = (key_block >= 0) & (key_block < block_count)
            key_start = (jnp.clip(key_block, 0, block_count - 1) * TOK_DEV).astype(jnp.int32)
            key_part = lax.dynamic_slice_in_dim(key_vectors, key_start, TOK_DEV, 0)
            value_part = lax.dynamic_slice_in_dim(value_vectors, key_start, TOK_DEV, 0)
            key_docs = lax.dynamic_slice_in_dim(all_docs, key_start, TOK_DEV, 0)
            intersections = in_range & (key_docs[0] <= query_docs[-1]) & (query_docs[0] <= key_docs[-1])

            def compute_terms():
                return pair_terms(query_part, grad_part, norm_part, delta_part, query_docs, key_part, value_part, key_docs, HEADS, HD)

            def zero_terms():
                blank = jnp.zeros((TOK_DEV, feat_count), jnp.float32)
                return (blank, blank, blank)

            query_add, key_add, value_add = lax.cond(intersections, compute_terms, zero_terms)
            query_total = query_total + query_add
            key_total = lax.dynamic_update_slice_in_dim(key_total, lax.dynamic_slice_in_dim(key_total, key_start, TOK_DEV, 0) + key_add, key_start, 0)
            value_total = lax.dynamic_update_slice_in_dim(value_total, lax.dynamic_slice_in_dim(value_total, key_start, TOK_DEV, 0) + value_add, key_start, 0)
        return (key_total, value_total), query_total.astype(jnp.bfloat16)

    start_totals = (jnp.zeros((TOKENS, feat_count), jnp.float32), jnp.zeros((TOKENS, feat_count), jnp.float32))
    (key_total, value_total), query_blocks = lax.scan(visit_block, start_totals, jnp.arange(block_count, dtype=jnp.int32))
    grad_queries = query_blocks.reshape(TOKENS, feat_count)
    return (grad_queries, key_total.astype(jnp.bfloat16), value_total.astype(jnp.bfloat16))
```

```python
import functools

import jax
import jax.numpy as jnp
from jax import lax
from jax.experimental import pallas as pl
from jax.experimental.pallas import tpu as pltpu
from jax.sharding import PartitionSpec as P

MESH = pl.DeviceIdType.MESH
CHUNK = 256


def row_docs(off_ref, position):
    doc = jnp.zeros(position.shape, jnp.int32)
    for slot in range(1, off_ref.shape[0]):
        doc = doc + jnp.where(position >= off_ref[slot], 1, 0)
    return doc


def contract_last(left, right):
    return lax.dot_general(
        left, right, (((1,), (1,)), ((), ())), preferred_element_type=jnp.float32
    )


def times(left, right):
    return jnp.dot(left, right, preferred_element_type=jnp.float32)


def kernel(
    reach,
    seq_count,
    head_devs,
    heads,
    q_ref,
    k_ref,
    v_ref,
    a_ref,
    o_ref,
    n_ref,
    off_ref,
    gq_ref,
    gk_ref,
    gv_ref,
    slot_q,
    slot_o,
    slot_s,
    own_s,
    own_dq,
    part,
    back,
    dk_acc,
    dv_acc,
    k_head,
    v_head,
    k_turned,
    key_doc,
    stage,
    send_sem,
    recv_sem,
    back_send,
    back_recv,
    out_send,
    out_recv,
):
    me = lax.axis_index("seq")
    col = lax.axis_index("head")
    rows, feats = q_ref.shape
    width = feats // heads
    slots = 2 * reach
    out_rows = rows // head_devs

    def offset(i):
        return (i // 2 + 1) * (1 - 2 * (i % 2))

    def mirror(i):
        return i + 1 - 2 * (i % 2)

    def inside(i):
        other = me + offset(i)
        return (other >= 0) & (other < seq_count)

    barrier = pltpu.get_barrier_semaphore()

    count = jnp.int32(head_devs - 1)
    for i in range(slots):
        count = count + inside(i).astype(jnp.int32)

        @pl.when(inside(i))
        def _(i=i):
            pl.semaphore_signal(
                barrier, inc=1, device_id=(me + offset(i), col), device_id_type=MESH
            )

    for step in range(1, head_devs):
        pl.semaphore_signal(
            barrier,
            inc=1,
            device_id=(me, lax.rem(col + step, head_devs)),
            device_id_type=MESH,
        )
    pl.semaphore_wait(barrier, count)

    def outgoing(i, which):
        src, dst = ((q_ref, slot_q), (o_ref, slot_o), (own_s, slot_s))[which]
        return pltpu.make_async_remote_copy(
            src_ref=src,
            dst_ref=dst.at[mirror(i)],
            send_sem=send_sem.at[i, which],
            recv_sem=recv_sem.at[mirror(i), which],
            device_id=(me + offset(i), col),
            device_id_type=MESH,
        )

    def incoming(i, which):
        src, dst = ((q_ref, slot_q), (o_ref, slot_o), (own_s, slot_s))[which]
        return pltpu.make_async_remote_copy(
            src_ref=src,
            dst_ref=dst.at[i],
            send_sem=send_sem.at[i, which],
            recv_sem=recv_sem.at[i, which],
            device_id=(me + offset(i), col),
            device_id_type=MESH,
        )

    def returning(i, slot):
        return pltpu.make_async_remote_copy(
            src_ref=part.at[i],
            dst_ref=back.at[slot],
            send_sem=back_send.at[i],
            recv_sem=back_recv.at[slot],
            device_id=(me + offset(i), col),
            device_id_type=MESH,
        )

    def start_out(i, _):
        @pl.when(inside(i))
        def _():
            outgoing(i, 0).start()
            outgoing(i, 1).start()

        return 0

    lax.fori_loop(0, slots, start_out, 0)

    product = o_ref[...].astype(jnp.float32) * a_ref[...].astype(jnp.float32)
    high = product.astype(jnp.bfloat16)
    low = (product - high.astype(jnp.float32)).astype(jnp.bfloat16)
    pick_row = lax.broadcasted_iota(jnp.int32, (8, feats), 0)
    pick_col = lax.broadcasted_iota(jnp.int32, (8, feats), 1)
    pick = jnp.where(pick_row - heads == pick_col // width, 1.0, 0.0).astype(jnp.bfloat16)
    own_s[...] = contract_last(pick, high) + contract_last(pick, low)
    own_s[0:heads, :] = n_ref[...]

    def start_stats(i, _):
        @pl.when(inside(i))
        def _():
            outgoing(i, 2).start()

        return 0

    lax.fori_loop(0, slots, start_stats, 0)

    scale = width ** (-0.5)
    keys = k_ref[...].astype(jnp.float32) * scale
    values = v_ref[...].astype(jnp.float32)
    lane = lax.broadcasted_iota(jnp.int32, (rows, feats), 1)
    for h in range(heads):
        mine = (lane >= h * width) & (lane < (h + 1) * width)
        k_head[h] = jnp.where(mine, keys, 0.0).astype(jnp.bfloat16)
        v_head[h] = jnp.where(mine, values, 0.0).astype(jnp.bfloat16)
    k_turned[...] = keys.T.astype(jnp.bfloat16)
    first = me * rows
    key_doc[...] = row_docs(
        off_ref, first + lax.broadcasted_iota(jnp.int32, key_doc.shape, 0)
    )
    dk_acc[...] = jnp.zeros_like(dk_acc)
    dv_acc[...] = jnp.zeros_like(dv_acc)

    def block(q_at, o_at, s_at, base, put):
        for c in range(rows // CHUNK):
            low_t = c * CHUNK
            span = slice(low_t, low_t + CHUNK)
            query = q_at[span, :]
            grad = o_at[span, :]
            query_doc = row_docs(
                off_ref, base + low_t + lax.broadcasted_iota(jnp.int32, (1, CHUNK), 1)
            )
            docs = jnp.concatenate([key_doc[...]] * (CHUNK // key_doc.shape[1]), axis=1)
            same = docs == query_doc
            lane_c = lax.broadcasted_iota(jnp.int32, (CHUNK, feats), 1)
            dk_add, dv_add = None, None
            for h in range(heads):
                mine = (lane_c >= h * width) & (lane_c < (h + 1) * width)
                score = contract_last(k_head[h], query)
                prob = jnp.where(same, jnp.exp(score - s_at[h : h + 1, span]), 0.0)
                gp = contract_last(v_head[h], grad)
                ds = (prob * (gp - s_at[heads + h : heads + h + 1, span])).astype(
                    jnp.bfloat16
                )
                query_h = jnp.where(mine, query, jnp.bfloat16(0))
                grad_h = jnp.where(mine, grad, jnp.bfloat16(0))
                dk_h = times(ds, query_h)
                dv_h = times(prob.astype(jnp.bfloat16), grad_h)
                dk_add = dk_h if dk_add is None else dk_add + dk_h
                dv_add = dv_h if dv_add is None else dv_add + dv_h
                put(h, span, times(k_turned[h * width : (h + 1) * width, :], ds))
            dk_acc[...] += dk_add
            dv_acc[...] += dv_add

    def put_own(h, span, value):
        own_dq[h * width : (h + 1) * width, span] = value

    block(q_ref, o_ref, own_s, first, put_own)

    def visit(i, _):
        @pl.when(inside(i))
        def _():
            for which in range(3):
                incoming(i, which).wait_recv()

            def put(h, span, value):
                part[i, h * width : (h + 1) * width, span] = value.astype(jnp.bfloat16)

            block(
                slot_q.at[i],
                slot_o.at[i],
                slot_s.at[i],
                (me + offset(i)) * rows,
                put,
            )
            returning(i, mirror(i)).start()

        return 0

    lax.fori_loop(0, slots, visit, 0)

    def sharing(which, step, into):
        out = (gq_ref, gk_ref, gv_ref)[which]
        partner = lax.rem(col + step, head_devs)
        column = col if into is None else into
        return pltpu.make_async_remote_copy(
            src_ref=stage.at[which, pl.ds(pl.multiple_of(partner * out_rows, out_rows), out_rows)],
            dst_ref=out.at[:, pl.ds(pl.multiple_of(column * feats, feats), feats)],
            send_sem=out_send.at[which, step - 1],
            recv_sem=out_recv.at[which, step - 1],
            device_id=(me, partner),
            device_id_type=MESH,
        )

    def share(which):
        for step in range(1, head_devs):
            sharing(which, step, None).start()
        out = (gq_ref, gk_ref, gv_ref)[which]
        out[:, pl.ds(pl.multiple_of(col * feats, feats), feats)] = stage[
            which, pl.ds(pl.multiple_of(col * out_rows, out_rows), out_rows), :
        ]

    stage[1] = (dk_acc[...] * scale).astype(jnp.bfloat16)
    stage[2] = dv_acc[...].astype(jnp.bfloat16)
    share(1)
    share(2)

    def gather(i, _):
        @pl.when(inside(i))
        def _():
            returning(i, i).wait_recv()
            own_dq[...] += back[i].astype(jnp.float32)

        return 0

    lax.fori_loop(0, slots, gather, 0)
    stage[0] = own_dq[...].T.astype(jnp.bfloat16)
    share(0)

    def finish(i, _):
        @pl.when(inside(i))
        def _():
            for which in range(3):
                outgoing(i, which).wait_send()
            returning(i, mirror(i)).wait_send()

        return 0

    lax.fori_loop(0, slots, finish, 0)
    for which in (1, 2, 0):
        for step in range(1, head_devs):
            copy = sharing(which, step, lax.rem(col + head_devs - step, head_devs))
            copy.wait_recv()
            copy.wait_send()


def on_device(seq_count, head_devs, *args):
    queries, log_norm = args[0], args[5]
    rows, feats = queries.shape
    heads = log_norm.shape[0]
    reach = min(8, seq_count // 4)
    slots = 2 * reach
    bf16, f32 = jnp.bfloat16, jnp.float32
    vmem = pl.BlockSpec(memory_space=pltpu.VMEM)
    out = jax.ShapeDtypeStruct((rows // head_devs, feats * head_devs), bf16)
    dma = pltpu.SemaphoreType.DMA
    return pl.pallas_call(
        functools.partial(kernel, reach, seq_count, head_devs, heads),
        out_shape=(out, out, out),
        in_specs=[vmem] * 6 + [pl.BlockSpec(memory_space=pltpu.SMEM)],
        out_specs=(vmem, vmem, vmem),
        scratch_shapes=[
            pltpu.VMEM((slots, rows, feats), bf16),
            pltpu.VMEM((slots, rows, feats), bf16),
            pltpu.VMEM((slots, 8, rows), f32),
            pltpu.VMEM((8, rows), f32),
            pltpu.VMEM((feats, rows), f32),
            pltpu.VMEM((slots, feats, rows), bf16),
            pltpu.VMEM((slots, feats, rows), bf16),
            pltpu.VMEM((rows, feats), f32),
            pltpu.VMEM((rows, feats), f32),
            pltpu.VMEM((heads, rows, feats), bf16),
            pltpu.VMEM((heads, rows, feats), bf16),
            pltpu.VMEM((feats, rows), bf16),
            pltpu.VMEM((rows, 128), jnp.int32),
            pltpu.VMEM((3, rows, feats), bf16),
            dma((slots, 3)),
            dma((slots, 3)),
            dma((slots,)),
            dma((slots,)),
            dma((3, head_devs - 1)),
            dma((3, head_devs - 1)),
        ],
        compiler_params=pltpu.CompilerParams(
            collective_id=0, has_side_effects=True, vmem_limit_bytes=40 * 1024 * 1024
        ),
    )(*args)


def solution(mesh):
    seq_count, head_devs = mesh.shape["seq"], mesh.shape["head"]
    in_specs = (
        P("seq", "head"),
        P("seq", "head"),
        P("seq", "head"),
        P("seq", "head"),
        P("seq", "head"),
        P("head", "seq"),
        P(),
    )
    out_specs = (P(("seq", "head"), None),) * 3
    return jax.shard_map(
        functools.partial(on_device, seq_count, head_devs),
        mesh=mesh,
        in_specs=in_specs,
        out_specs=out_specs,
        check_vma=False,
    )
```

```python
import functools

import jax
import jax.numpy as jnp
from jax import lax
from jax.experimental import pallas as pl
from jax.experimental.pallas import tpu as pltpu
from jax.sharding import PartitionSpec as P

MESH = pl.DeviceIdType.MESH
CHUNK = 256


def row_docs(off_ref, position):
    doc = jnp.zeros(position.shape, jnp.int32)
    for slot in range(1, off_ref.shape[0]):
        doc = doc + jnp.where(position >= off_ref[slot], 1, 0)
    return doc


def contract_last(left, right):
    return lax.dot_general(
        left, right, (((1,), (1,)), ((), ())), preferred_element_type=jnp.float32
    )


def times(left, right):
    return jnp.dot(left, right, preferred_element_type=jnp.float32)


def kernel(
    reach,
    seq_count,
    head_devs,
    heads,
    q_hbm,
    k_hbm,
    v_hbm,
    a_hbm,
    o_hbm,
    n_hbm,
    off_hbm,
    gq_ref,
    gk_ref,
    gv_ref,
    q_ref,
    k_ref,
    v_ref,
    a_ref,
    o_ref,
    n_ref,
    off_ref,
    load_sem,
    slot_q,
    slot_o,
    slot_s,
    own_s,
    own_dq,
    part,
    back,
    dk_acc,
    dv_acc,
    k_head,
    v_head,
    k_turned,
    key_doc,
    stage,
    send_sem,
    recv_sem,
    back_send,
    back_recv,
    out_send,
    out_recv,
    keep_sem,
):
    me = lax.axis_index("seq")
    col = lax.axis_index("head")
    rows, feats = q_ref.shape
    width = feats // heads
    slots = 2 * reach
    out_rows = rows // head_devs

    def offset(i):
        return (i // 2 + 1) * (1 - 2 * (i % 2))

    def mirror(i):
        return i + 1 - 2 * (i % 2)

    def inside(i):
        other = me + offset(i)
        return (other >= 0) & (other < seq_count)

    loads = [
        pltpu.make_async_copy(src, dst, load_sem.at[i])
        for i, (src, dst) in enumerate(
            (
                (o_hbm, o_ref),
                (a_hbm, a_ref),
                (n_hbm, n_ref),
                (off_hbm, off_ref),
                (k_hbm, k_ref),
                (v_hbm, v_ref),
                (q_hbm, q_ref),
            )
        )
    ]
    for load in loads:
        load.start()

    barrier = pltpu.get_barrier_semaphore()

    count = jnp.int32(head_devs - 1)
    for i in range(slots):
        count = count + inside(i).astype(jnp.int32)

        @pl.when(inside(i))
        def _(i=i):
            pl.semaphore_signal(
                barrier, inc=1, device_id=(me + offset(i), col), device_id_type=MESH
            )

    for step in range(1, head_devs):
        pl.semaphore_signal(
            barrier,
            inc=1,
            device_id=(me, lax.rem(col + step, head_devs)),
            device_id_type=MESH,
        )
    pl.semaphore_wait(barrier, count)

    def outgoing(i, which):
        src, dst = ((q_hbm, slot_q), (o_hbm, slot_o), (own_s, slot_s))[which]
        return pltpu.make_async_remote_copy(
            src_ref=src,
            dst_ref=dst.at[mirror(i)],
            send_sem=send_sem.at[i, which],
            recv_sem=recv_sem.at[mirror(i), which],
            device_id=(me + offset(i), col),
            device_id_type=MESH,
        )

    def incoming(i, which):
        src, dst = ((q_hbm, slot_q), (o_hbm, slot_o), (own_s, slot_s))[which]
        return pltpu.make_async_remote_copy(
            src_ref=src,
            dst_ref=dst.at[i],
            send_sem=send_sem.at[i, which],
            recv_sem=recv_sem.at[i, which],
            device_id=(me + offset(i), col),
            device_id_type=MESH,
        )

    def returning(i, slot):
        return pltpu.make_async_remote_copy(
            src_ref=part.at[i],
            dst_ref=back.at[slot],
            send_sem=back_send.at[i],
            recv_sem=back_recv.at[slot],
            device_id=(me + offset(i), col),
            device_id_type=MESH,
        )

    def start_out(i, _):
        @pl.when(inside(i))
        def _():
            outgoing(i, 0).start()
            outgoing(i, 1).start()

        return 0

    lax.fori_loop(0, slots, start_out, 0)

    for load in loads[:3]:
        load.wait()
    product = o_ref[...].astype(jnp.float32) * a_ref[...].astype(jnp.float32)
    high = product.astype(jnp.bfloat16)
    low = (product - high.astype(jnp.float32)).astype(jnp.bfloat16)
    pick_row = lax.broadcasted_iota(jnp.int32, (8, feats), 0)
    pick_col = lax.broadcasted_iota(jnp.int32, (8, feats), 1)
    pick = jnp.where(pick_row - heads == pick_col // width, 1.0, 0.0).astype(jnp.bfloat16)
    own_s[...] = contract_last(pick, high) + contract_last(pick, low)
    own_s[0:heads, :] = n_ref[...]

    def start_stats(i, _):
        @pl.when(inside(i))
        def _():
            outgoing(i, 2).start()

        return 0

    lax.fori_loop(0, slots, start_stats, 0)

    for load in loads[3:]:
        load.wait()
    scale = width ** (-0.5)
    keys = k_ref[...].astype(jnp.float32) * scale
    values = v_ref[...].astype(jnp.float32)
    lane = lax.broadcasted_iota(jnp.int32, (rows, feats), 1)
    for h in range(heads):
        mine = (lane >= h * width) & (lane < (h + 1) * width)
        k_head[h] = jnp.where(mine, keys, 0.0).astype(jnp.bfloat16)
        v_head[h] = jnp.where(mine, values, 0.0).astype(jnp.bfloat16)
    k_turned[...] = keys.T.astype(jnp.bfloat16)
    first = me * rows
    key_doc[...] = row_docs(
        off_ref, first + lax.broadcasted_iota(jnp.int32, key_doc.shape, 0)
    )
    dk_acc[...] = jnp.zeros_like(dk_acc)
    dv_acc[...] = jnp.zeros_like(dv_acc)

    def block(q_at, o_at, s_at, base, put):
        for c in range(rows // CHUNK):
            low_t = c * CHUNK
            span = slice(low_t, low_t + CHUNK)
            query = q_at[span, :]
            grad = o_at[span, :]
            query_doc = row_docs(
                off_ref, base + low_t + lax.broadcasted_iota(jnp.int32, (1, CHUNK), 1)
            )
            docs = jnp.concatenate([key_doc[...]] * (CHUNK // key_doc.shape[1]), axis=1)
            same = docs == query_doc
            lane_c = lax.broadcasted_iota(jnp.int32, (CHUNK, feats), 1)
            dk_add, dv_add = None, None
            for h in range(heads):
                mine = (lane_c >= h * width) & (lane_c < (h + 1) * width)
                score = contract_last(k_head[h], query)
                prob = jnp.where(same, jnp.exp(score - s_at[h : h + 1, span]), 0.0)
                gp = contract_last(v_head[h], grad)
                ds = (prob * (gp - s_at[heads + h : heads + h + 1, span])).astype(
                    jnp.bfloat16
                )
                query_h = jnp.where(mine, query, jnp.bfloat16(0))
                grad_h = jnp.where(mine, grad, jnp.bfloat16(0))
                dk_h = times(ds, query_h)
                dv_h = times(prob.astype(jnp.bfloat16), grad_h)
                dk_add = dk_h if dk_add is None else dk_add + dk_h
                dv_add = dv_h if dv_add is None else dv_add + dv_h
                put(h, span, times(k_turned[h * width : (h + 1) * width, :], ds))
            dk_acc[...] += dk_add
            dv_acc[...] += dv_add

    def put_own(h, span, value):
        own_dq[h * width : (h + 1) * width, span] = value

    block(q_ref, o_ref, own_s, first, put_own)

    def visit(i, _):
        @pl.when(inside(i))
        def _():
            for which in range(3):
                incoming(i, which).wait_recv()

            def put(h, span, value):
                part[i, h * width : (h + 1) * width, span] = value.astype(jnp.bfloat16)

            block(
                slot_q.at[i],
                slot_o.at[i],
                slot_s.at[i],
                (me + offset(i)) * rows,
                put,
            )
            returning(i, mirror(i)).start()

        return 0

    lax.fori_loop(0, slots, visit, 0)

    def sharing(which, step, into):
        out = (gq_ref, gk_ref, gv_ref)[which]
        partner = lax.rem(col + step, head_devs)
        column = col if into is None else into
        return pltpu.make_async_remote_copy(
            src_ref=stage.at[which, pl.ds(pl.multiple_of(partner * out_rows, out_rows), out_rows)],
            dst_ref=out.at[:, pl.ds(pl.multiple_of(column * feats, feats), feats)],
            send_sem=out_send.at[which, step - 1],
            recv_sem=out_recv.at[which, step - 1],
            device_id=(me, partner),
            device_id_type=MESH,
        )

    def keeping(which):
        out = (gq_ref, gk_ref, gv_ref)[which]
        return pltpu.make_async_copy(
            stage.at[which, pl.ds(pl.multiple_of(col * out_rows, out_rows), out_rows)],
            out.at[:, pl.ds(pl.multiple_of(col * feats, feats), feats)],
            keep_sem.at[which],
        )

    def share(which):
        for step in range(1, head_devs):
            sharing(which, step, None).start()
        keeping(which).start()

    stage[1] = (dk_acc[...] * scale).astype(jnp.bfloat16)
    stage[2] = dv_acc[...].astype(jnp.bfloat16)
    share(1)
    share(2)

    def gather(i, _):
        @pl.when(inside(i))
        def _():
            returning(i, i).wait_recv()
            own_dq[...] += back[i].astype(jnp.float32)

        return 0

    lax.fori_loop(0, slots, gather, 0)
    stage[0] = own_dq[...].T.astype(jnp.bfloat16)
    share(0)

    def finish(i, _):
        @pl.when(inside(i))
        def _():
            for which in range(3):
                outgoing(i, which).wait_send()
            returning(i, mirror(i)).wait_send()

        return 0

    lax.fori_loop(0, slots, finish, 0)
    for which in (1, 2, 0):
        keeping(which).wait()
        for step in range(1, head_devs):
            copy = sharing(which, step, lax.rem(col + head_devs - step, head_devs))
            copy.wait_recv()
            copy.wait_send()


def on_device(seq_count, head_devs, *args):
    queries, log_norm = args[0], args[5]
    rows, feats = queries.shape
    heads = log_norm.shape[0]
    reach = min(8, seq_count // 4)
    slots = 2 * reach
    bf16, f32 = jnp.bfloat16, jnp.float32
    hbm = pl.BlockSpec(memory_space=pltpu.HBM)
    out = jax.ShapeDtypeStruct((rows // head_devs, feats * head_devs), bf16)
    dma = pltpu.SemaphoreType.DMA
    results = pl.pallas_call(
        functools.partial(kernel, reach, seq_count, head_devs, heads),
        out_shape=(out, out, out),
        in_specs=[hbm] * 7,
        out_specs=(hbm,) * 3,
        scratch_shapes=[
            *[pltpu.VMEM((rows, feats), bf16)] * 5,
            pltpu.VMEM(log_norm.shape, f32),
            pltpu.SMEM(args[6].shape, jnp.int32),
            dma((7,)),
            pltpu.VMEM((slots, rows, feats), bf16),
            pltpu.VMEM((slots, rows, feats), bf16),
            pltpu.VMEM((slots, 8, rows), f32),
            pltpu.VMEM((8, rows), f32),
            pltpu.VMEM((feats, rows), f32),
            pltpu.VMEM((slots, feats, rows), bf16),
            pltpu.VMEM((slots, feats, rows), bf16),
            pltpu.VMEM((rows, feats), f32),
            pltpu.VMEM((rows, feats), f32),
            pltpu.VMEM((heads, rows, feats), bf16),
            pltpu.VMEM((heads, rows, feats), bf16),
            pltpu.VMEM((feats, rows), bf16),
            pltpu.VMEM((rows, 128), jnp.int32),
            pltpu.VMEM((3, rows, feats), bf16),
            dma((slots, 3)),
            dma((slots, 3)),
            dma((slots,)),
            dma((slots,)),
            dma((3, head_devs - 1)),
            dma((3, head_devs - 1)),
            dma((3,)),
        ],
        compiler_params=pltpu.CompilerParams(
            collective_id=0, has_side_effects=True
        ),
    )(*args)
    vmem = pl.BlockSpec(memory_space=pltpu.VMEM)
    return pl.pallas_call(
        hand_over,
        out_shape=(out,) * 3,
        in_specs=[vmem] * 3,
        out_specs=(hbm,) * 3,
        scratch_shapes=[dma((3,))],
    )(*results)


def hand_over(*refs):
    sem = refs[6]
    copies = [pltpu.make_async_copy(refs[i], refs[3 + i], sem.at[i]) for i in range(3)]
    for copy in copies:
        copy.start()
    for copy in copies:
        copy.wait()


def solution(mesh):
    seq_count, head_devs = mesh.shape["seq"], mesh.shape["head"]
    in_specs = (
        P("seq", "head"),
        P("seq", "head"),
        P("seq", "head"),
        P("seq", "head"),
        P("seq", "head"),
        P("head", "seq"),
        P(),
    )
    out_specs = (P(("seq", "head"), None),) * 3
    return jax.shard_map(
        functools.partial(on_device, seq_count, head_devs),
        mesh=mesh,
        in_specs=in_specs,
        out_specs=out_specs,
        check_vma=False,
    )
```

```python
import functools

import jax
import jax.numpy as jnp
from jax import lax
from jax.experimental import pallas as pl
from jax.experimental.pallas import tpu as pltpu
from jax.sharding import PartitionSpec as P

MESH = pl.DeviceIdType.MESH
CHUNK = 256


def row_docs(off_ref, position):
    doc = jnp.zeros(position.shape, jnp.int32)
    for slot in range(1, off_ref.shape[0]):
        doc = doc + jnp.where(position >= off_ref[slot], 1, 0)
    return doc


def contract_last(left, right):
    return lax.dot_general(
        left, right, (((1,), (1,)), ((), ())), preferred_element_type=jnp.float32
    )


def times(left, right):
    return jnp.dot(left, right, preferred_element_type=jnp.float32)


def kernel(
    reach,
    seq_count,
    head_devs,
    heads,
    q_hbm,
    k_hbm,
    v_hbm,
    a_hbm,
    o_hbm,
    n_hbm,
    off_hbm,
    gq_ref,
    gk_ref,
    gv_ref,
    q_ref,
    k_ref,
    v_ref,
    a_ref,
    o_ref,
    n_ref,
    off_ref,
    load_sem,
    slot_q,
    slot_o,
    slot_s,
    own_s,
    own_dq,
    part,
    back,
    dk_acc,
    dv_acc,
    k_head,
    v_head,
    k_turned,
    key_doc,
    stage,
    send_sem,
    recv_sem,
    back_send,
    back_recv,
    out_send,
    out_recv,
    keep_sem,
    relay_send,
):
    me = lax.axis_index("seq")
    col = lax.axis_index("head")
    rows, feats = q_ref.shape
    width = feats // heads
    slots = 2 * reach
    out_rows = rows // head_devs

    def offset(i):
        return (i // 2 + 1) * (1 - 2 * (i % 2))

    def mirror(i):
        return i + 1 - 2 * (i % 2)

    def inside(i):
        other = me + offset(i)
        return (other >= 0) & (other < seq_count)

    loads = [
        pltpu.make_async_copy(src, dst, load_sem.at[i])
        for i, (src, dst) in enumerate(
            (
                (o_hbm, o_ref),
                (a_hbm, a_ref),
                (n_hbm, n_ref),
                (off_hbm, off_ref),
                (k_hbm, k_ref),
                (v_hbm, v_ref),
                (q_hbm, q_ref),
            )
        )
    ]
    for load in loads:
        load.start()

    barrier = pltpu.get_barrier_semaphore()

    count = jnp.int32(head_devs - 1)
    for i in range(slots):
        count = count + inside(i).astype(jnp.int32)

        @pl.when(inside(i))
        def _(i=i):
            pl.semaphore_signal(
                barrier, inc=1, device_id=(me + offset(i), col), device_id_type=MESH
            )

    for step in range(1, head_devs):
        pl.semaphore_signal(
            barrier,
            inc=1,
            device_id=(me, lax.rem(col + step, head_devs)),
            device_id_type=MESH,
        )
    pl.semaphore_wait(barrier, count)

    def outgoing(i, which):
        src, dst = ((q_hbm, slot_q), (o_hbm, slot_o), (own_s, slot_s))[which]
        return pltpu.make_async_remote_copy(
            src_ref=src,
            dst_ref=dst.at[mirror(i)],
            send_sem=send_sem.at[i, which],
            recv_sem=recv_sem.at[mirror(i), which],
            device_id=(me + offset(i), col),
            device_id_type=MESH,
        )

    def incoming(i, which):
        src, dst = ((q_hbm, slot_q), (o_hbm, slot_o), (own_s, slot_s))[which]
        return pltpu.make_async_remote_copy(
            src_ref=src,
            dst_ref=dst.at[i],
            send_sem=send_sem.at[i, which],
            recv_sem=recv_sem.at[i, which],
            device_id=(me + offset(i), col),
            device_id_type=MESH,
        )

    def returning(i, slot):
        return pltpu.make_async_remote_copy(
            src_ref=part.at[i],
            dst_ref=back.at[slot],
            send_sem=back_send.at[i],
            recv_sem=back_recv.at[slot],
            device_id=(me + offset(i), col),
            device_id_type=MESH,
        )

    odd = lax.rem(me, 2)
    direct, diagonal = odd, 1 - odd
    ahead, behind = 2 + odd, 3 - odd

    def when_inside(i, act):
        @pl.when(inside(i))
        def _():
            act()

    def relay_q():
        return pltpu.make_async_remote_copy(
            src_ref=slot_q.at[direct],
            dst_ref=slot_q.at[diagonal],
            send_sem=relay_send.at[0],
            recv_sem=recv_sem.at[diagonal, 0],
            device_id=(me + offset(ahead), col),
            device_id_type=MESH,
        )

    def relay_o():
        return pltpu.make_async_remote_copy(
            src_ref=slot_o.at[ahead],
            dst_ref=slot_o.at[odd],
            send_sem=relay_send.at[1],
            recv_sem=recv_sem.at[odd, 1],
            device_id=(me + offset(direct), col),
            device_id_type=MESH,
        )

    outgoing(direct, 0).start()
    when_inside(behind, lambda: outgoing(behind, 1).start())
    outgoing(direct, 1).start()
    when_inside(behind, lambda: outgoing(behind, 0).start())

    def send_ahead():
        outgoing(ahead, 0).start()
        outgoing(ahead, 1).start()

    when_inside(ahead, send_ahead)

    def start_out(i, _):
        @pl.when(inside(i))
        def _():
            outgoing(i, 0).start()
            outgoing(i, 1).start()

        return 0

    lax.fori_loop(4, slots, start_out, 0)

    for load in loads[:3]:
        load.wait()
    product = o_ref[...].astype(jnp.float32) * a_ref[...].astype(jnp.float32)
    high = product.astype(jnp.bfloat16)
    low = (product - high.astype(jnp.float32)).astype(jnp.bfloat16)
    pick_row = lax.broadcasted_iota(jnp.int32, (8, feats), 0)
    pick_col = lax.broadcasted_iota(jnp.int32, (8, feats), 1)
    pick = jnp.where(pick_row - heads == pick_col // width, 1.0, 0.0).astype(jnp.bfloat16)
    own_s[...] = contract_last(pick, high) + contract_last(pick, low)
    own_s[0:heads, :] = n_ref[...]

    def start_stats(i, _):
        @pl.when(inside(i))
        def _():
            outgoing(i, 2).start()

        return 0

    lax.fori_loop(0, slots, start_stats, 0)

    for load in loads[3:]:
        load.wait()
    scale = width ** (-0.5)
    keys = k_ref[...].astype(jnp.float32) * scale
    values = v_ref[...].astype(jnp.float32)
    lane = lax.broadcasted_iota(jnp.int32, (rows, feats), 1)
    for h in range(heads):
        mine = (lane >= h * width) & (lane < (h + 1) * width)
        k_head[h] = jnp.where(mine, keys, 0.0).astype(jnp.bfloat16)
        v_head[h] = jnp.where(mine, values, 0.0).astype(jnp.bfloat16)
    k_turned[...] = keys.T.astype(jnp.bfloat16)
    first = me * rows
    key_doc[...] = row_docs(
        off_ref, first + lax.broadcasted_iota(jnp.int32, key_doc.shape, 0)
    )
    dk_acc[...] = jnp.zeros_like(dk_acc)
    dv_acc[...] = jnp.zeros_like(dv_acc)

    def block(q_at, o_at, s_at, base, put):
        for c in range(rows // CHUNK):
            low_t = c * CHUNK
            span = slice(low_t, low_t + CHUNK)
            query = q_at[span, :]
            grad = o_at[span, :]
            query_doc = row_docs(
                off_ref, base + low_t + lax.broadcasted_iota(jnp.int32, (1, CHUNK), 1)
            )
            docs = jnp.concatenate([key_doc[...]] * (CHUNK // key_doc.shape[1]), axis=1)
            same = docs == query_doc
            lane_c = lax.broadcasted_iota(jnp.int32, (CHUNK, feats), 1)
            dk_add, dv_add = None, None
            for h in range(heads):
                mine = (lane_c >= h * width) & (lane_c < (h + 1) * width)
                score = contract_last(k_head[h], query)
                prob = jnp.where(same, jnp.exp(score - s_at[h : h + 1, span]), 0.0)
                gp = contract_last(v_head[h], grad)
                ds = (prob * (gp - s_at[heads + h : heads + h + 1, span])).astype(
                    jnp.bfloat16
                )
                query_h = jnp.where(mine, query, jnp.bfloat16(0))
                grad_h = jnp.where(mine, grad, jnp.bfloat16(0))
                dk_h = times(ds, query_h)
                dv_h = times(prob.astype(jnp.bfloat16), grad_h)
                dk_add = dk_h if dk_add is None else dk_add + dk_h
                dv_add = dv_h if dv_add is None else dv_add + dv_h
                put(h, span, times(k_turned[h * width : (h + 1) * width, :], ds))
            dk_acc[...] += dk_add
            dv_acc[...] += dv_add

    def put_own(h, span, value):
        own_dq[h * width : (h + 1) * width, span] = value

    block(q_ref, o_ref, own_s, first, put_own)

    def relay():
        incoming(ahead, 1).wait_recv()
        relay_o().start()

    incoming(direct, 0).wait_recv()
    when_inside(ahead, lambda: relay_q().start())
    when_inside(ahead, relay)

    def visit(i, waits):
        for which in waits:
            incoming(i, which).wait_recv()

        def put(h, span, value):
            part[i, h * width : (h + 1) * width, span] = value.astype(jnp.bfloat16)

        block(slot_q.at[i], slot_o.at[i], slot_s.at[i], (me + offset(i)) * rows, put)
        returning(i, mirror(i)).start()

    def visit_rest(i, _):
        when_inside(i, lambda: visit(i, (0, 1, 2)))
        return 0

    visit(direct, (1, 2))
    when_inside(ahead, lambda: visit(ahead, (0, 2)))
    when_inside(behind, lambda: visit(behind, (0, 1, 2)))
    when_inside(diagonal, lambda: visit(diagonal, (0, 1, 2)))
    lax.fori_loop(4, slots, visit_rest, 0)

    def sharing(which, step, into):
        out = (gq_ref, gk_ref, gv_ref)[which]
        partner = lax.rem(col + step, head_devs)
        column = col if into is None else into
        return pltpu.make_async_remote_copy(
            src_ref=stage.at[which, pl.ds(pl.multiple_of(partner * out_rows, out_rows), out_rows)],
            dst_ref=out.at[:, pl.ds(pl.multiple_of(column * feats, feats), feats)],
            send_sem=out_send.at[which, step - 1],
            recv_sem=out_recv.at[which, step - 1],
            device_id=(me, partner),
            device_id_type=MESH,
        )

    def keeping(which):
        out = (gq_ref, gk_ref, gv_ref)[which]
        return pltpu.make_async_copy(
            stage.at[which, pl.ds(pl.multiple_of(col * out_rows, out_rows), out_rows)],
            out.at[:, pl.ds(pl.multiple_of(col * feats, feats), feats)],
            keep_sem.at[which],
        )

    def share(which):
        for step in range(1, head_devs):
            sharing(which, step, None).start()
        keeping(which).start()

    stage[1] = (dk_acc[...] * scale).astype(jnp.bfloat16)
    stage[2] = dv_acc[...].astype(jnp.bfloat16)
    share(1)
    share(2)

    def gather(i, _):
        @pl.when(inside(i))
        def _():
            returning(i, i).wait_recv()
            own_dq[...] += back[i].astype(jnp.float32)

        return 0

    lax.fori_loop(0, slots, gather, 0)
    stage[0] = own_dq[...].T.astype(jnp.bfloat16)
    share(0)

    def finish(i, _):
        @pl.when(inside(i))
        def _():
            for which in range(3):
                outgoing(i, which).wait_send()
            returning(i, mirror(i)).wait_send()

        return 0

    def finish_diagonal():
        outgoing(diagonal, 2).wait_send()
        returning(diagonal, mirror(diagonal)).wait_send()

    def finish_relay():
        relay_q().wait_send()
        relay_o().wait_send()

    finish(direct, 0)
    when_inside(diagonal, finish_diagonal)
    when_inside(ahead, finish_relay)
    lax.fori_loop(2, slots, finish, 0)
    for which in (1, 2, 0):
        keeping(which).wait()
        for step in range(1, head_devs):
            copy = sharing(which, step, lax.rem(col + head_devs - step, head_devs))
            copy.wait_recv()
            copy.wait_send()


def on_device(seq_count, head_devs, *args):
    queries, log_norm = args[0], args[5]
    rows, feats = queries.shape
    heads = log_norm.shape[0]
    reach = min(8, seq_count // 4)
    slots = 2 * reach
    bf16, f32 = jnp.bfloat16, jnp.float32
    hbm = pl.BlockSpec(memory_space=pltpu.HBM)
    out = jax.ShapeDtypeStruct((rows // head_devs, feats * head_devs), bf16)
    dma = pltpu.SemaphoreType.DMA
    results = pl.pallas_call(
        functools.partial(kernel, reach, seq_count, head_devs, heads),
        out_shape=(out, out, out),
        in_specs=[hbm] * 7,
        out_specs=(hbm,) * 3,
        scratch_shapes=[
            *[pltpu.VMEM((rows, feats), bf16)] * 5,
            pltpu.VMEM(log_norm.shape, f32),
            pltpu.SMEM(args[6].shape, jnp.int32),
            dma((7,)),
            pltpu.VMEM((slots, rows, feats), bf16),
            pltpu.VMEM((slots, rows, feats), bf16),
            pltpu.VMEM((slots, 8, rows), f32),
            pltpu.VMEM((8, rows), f32),
            pltpu.VMEM((feats, rows), f32),
            pltpu.VMEM((slots, feats, rows), bf16),
            pltpu.VMEM((slots, feats, rows), bf16),
            pltpu.VMEM((rows, feats), f32),
            pltpu.VMEM((rows, feats), f32),
            pltpu.VMEM((heads, rows, feats), bf16),
            pltpu.VMEM((heads, rows, feats), bf16),
            pltpu.VMEM((feats, rows), bf16),
            pltpu.VMEM((rows, 128), jnp.int32),
            pltpu.VMEM((3, rows, feats), bf16),
            dma((slots, 3)),
            dma((slots, 3)),
            dma((slots,)),
            dma((slots,)),
            dma((3, head_devs - 1)),
            dma((3, head_devs - 1)),
            dma((3,)),
            dma((2,)),
        ],
        compiler_params=pltpu.CompilerParams(
            collective_id=0, has_side_effects=True
        ),
    )(*args)
    vmem = pl.BlockSpec(memory_space=pltpu.VMEM)
    return pl.pallas_call(
        hand_over,
        out_shape=(out,) * 3,
        in_specs=[vmem] * 3,
        out_specs=(hbm,) * 3,
        scratch_shapes=[dma((3,))],
    )(*results)


def hand_over(*refs):
    sem = refs[6]
    copies = [pltpu.make_async_copy(refs[i], refs[3 + i], sem.at[i]) for i in range(3)]
    for copy in copies:
        copy.start()
    for copy in copies:
        copy.wait()


def solution(mesh):
    seq_count, head_devs = mesh.shape["seq"], mesh.shape["head"]
    in_specs = (
        P("seq", "head"),
        P("seq", "head"),
        P("seq", "head"),
        P("seq", "head"),
        P("seq", "head"),
        P("head", "seq"),
        P(),
    )
    out_specs = (P(("seq", "head"), None),) * 3
    return jax.shard_map(
        functools.partial(on_device, seq_count, head_devs),
        mesh=mesh,
        in_specs=in_specs,
        out_specs=out_specs,
        check_vma=False,
    )
```

```python
import functools

import jax
import jax.numpy as jnp
from jax import lax
from jax.experimental import pallas as pl
from jax.experimental.pallas import tpu as pltpu
from jax.sharding import PartitionSpec as P

MESH = pl.DeviceIdType.MESH
CHUNK = 256


def row_docs(off_ref, position):
    doc = jnp.zeros(position.shape, jnp.int32)
    for slot in range(1, off_ref.shape[0]):
        doc = doc + jnp.where(position >= off_ref[slot], 1, 0)
    return doc


def contract_last(left, right):
    return lax.dot_general(
        left, right, (((1,), (1,)), ((), ())), preferred_element_type=jnp.float32
    )


def times(left, right):
    return jnp.dot(left, right, preferred_element_type=jnp.float32)


def kernel(
    reach,
    seq_count,
    head_devs,
    heads,
    q_hbm,
    k_hbm,
    v_hbm,
    a_hbm,
    o_hbm,
    n_hbm,
    off_hbm,
    gq_ref,
    gk_ref,
    gv_ref,
    q_ref,
    k_ref,
    v_ref,
    a_ref,
    o_ref,
    n_ref,
    off_ref,
    load_sem,
    slot_q,
    slot_o,
    slot_s,
    own_s,
    own_dq,
    part,
    back,
    dk_acc,
    dv_acc,
    k_head,
    v_head,
    k_turned,
    key_doc,
    stage,
    send_sem,
    recv_sem,
    back_send,
    back_recv,
    out_send,
    out_recv,
    keep_sem,
    relay_send,
):
    me = lax.axis_index("seq")
    col = lax.axis_index("head")
    rows, feats = q_ref.shape
    width = feats // heads
    slots = 2 * reach
    out_rows = rows // head_devs

    def offset(i):
        return (i // 2 + 1) * (1 - 2 * (i % 2))

    def mirror(i):
        return i + 1 - 2 * (i % 2)

    def inside(i):
        other = me + offset(i)
        return (other >= 0) & (other < seq_count)

    loads = [
        pltpu.make_async_copy(src, dst, load_sem.at[i])
        for i, (src, dst) in enumerate(
            (
                (o_hbm, o_ref),
                (a_hbm, a_ref),
                (n_hbm, n_ref),
                (off_hbm, off_ref),
                (k_hbm, k_ref),
                (v_hbm, v_ref),
                (q_hbm, q_ref),
            )
        )
    ]
    for load in loads:
        load.start()

    barrier = pltpu.get_barrier_semaphore()

    count = jnp.int32(head_devs - 1)
    for i in range(slots):
        count = count + inside(i).astype(jnp.int32)

        @pl.when(inside(i))
        def _(i=i):
            pl.semaphore_signal(
                barrier, inc=1, device_id=(me + offset(i), col), device_id_type=MESH
            )

    for step in range(1, head_devs):
        pl.semaphore_signal(
            barrier,
            inc=1,
            device_id=(me, lax.rem(col + step, head_devs)),
            device_id_type=MESH,
        )
    pl.semaphore_wait(barrier, count)

    def outgoing(i, which):
        src, dst = ((q_hbm, slot_q), (o_hbm, slot_o), (own_s, slot_s))[which]
        return pltpu.make_async_remote_copy(
            src_ref=src,
            dst_ref=dst.at[mirror(i)],
            send_sem=send_sem.at[i, which],
            recv_sem=recv_sem.at[mirror(i), which],
            device_id=(me + offset(i), col),
            device_id_type=MESH,
        )

    def incoming(i, which):
        src, dst = ((q_hbm, slot_q), (o_hbm, slot_o), (own_s, slot_s))[which]
        return pltpu.make_async_remote_copy(
            src_ref=src,
            dst_ref=dst.at[i],
            send_sem=send_sem.at[i, which],
            recv_sem=recv_sem.at[i, which],
            device_id=(me + offset(i), col),
            device_id_type=MESH,
        )

    def returning(i, slot):
        return pltpu.make_async_remote_copy(
            src_ref=part.at[i],
            dst_ref=back.at[slot],
            send_sem=back_send.at[i],
            recv_sem=back_recv.at[slot],
            device_id=(me + offset(i), col),
            device_id_type=MESH,
        )

    odd = lax.rem(me, 2)
    direct, diagonal = odd, 1 - odd
    ahead, behind = 2 + odd, 3 - odd

    def when_inside(i, act):
        @pl.when(inside(i))
        def _():
            act()

    def relay_q():
        return pltpu.make_async_remote_copy(
            src_ref=slot_q.at[direct],
            dst_ref=slot_q.at[diagonal],
            send_sem=relay_send.at[0],
            recv_sem=recv_sem.at[diagonal, 0],
            device_id=(me + offset(ahead), col),
            device_id_type=MESH,
        )

    def relay_o():
        return pltpu.make_async_remote_copy(
            src_ref=slot_o.at[ahead],
            dst_ref=slot_o.at[odd],
            send_sem=relay_send.at[1],
            recv_sem=recv_sem.at[odd, 1],
            device_id=(me + offset(direct), col),
            device_id_type=MESH,
        )

    outgoing(direct, 0).start()
    when_inside(behind, lambda: outgoing(behind, 1).start())
    outgoing(direct, 1).start()
    when_inside(behind, lambda: outgoing(behind, 0).start())

    def send_ahead():
        outgoing(ahead, 0).start()
        outgoing(ahead, 1).start()

    when_inside(ahead, send_ahead)

    def start_out(i, _):
        @pl.when(inside(i))
        def _():
            outgoing(i, 0).start()
            outgoing(i, 1).start()

        return 0

    lax.fori_loop(4, slots, start_out, 0)

    for load in loads[:3]:
        load.wait()
    product = o_ref[...].astype(jnp.float32) * a_ref[...].astype(jnp.float32)
    high = product.astype(jnp.bfloat16)
    low = (product - high.astype(jnp.float32)).astype(jnp.bfloat16)
    pick_row = lax.broadcasted_iota(jnp.int32, (8, feats), 0)
    pick_col = lax.broadcasted_iota(jnp.int32, (8, feats), 1)
    pick = jnp.where(pick_row - heads == pick_col // width, 1.0, 0.0).astype(jnp.bfloat16)
    own_s[...] = contract_last(pick, high) + contract_last(pick, low)
    own_s[0:heads, :] = n_ref[...]

    def start_stats(i, _):
        @pl.when(inside(i))
        def _():
            outgoing(i, 2).start()

        return 0

    lax.fori_loop(0, slots, start_stats, 0)

    for load in loads[3:]:
        load.wait()
    scale = width ** (-0.5)
    keys = k_ref[...].astype(jnp.float32) * scale
    values = v_ref[...].astype(jnp.float32)
    lane = lax.broadcasted_iota(jnp.int32, (rows, feats), 1)
    for h in range(heads):
        mine = (lane >= h * width) & (lane < (h + 1) * width)
        k_head[h] = jnp.where(mine, keys, 0.0).astype(jnp.bfloat16)
        v_head[h] = jnp.where(mine, values, 0.0).astype(jnp.bfloat16)
    k_turned[...] = keys.T.astype(jnp.bfloat16)
    first = me * rows
    key_doc[...] = row_docs(
        off_ref, first + lax.broadcasted_iota(jnp.int32, key_doc.shape, 0)
    )
    dk_acc[...] = jnp.zeros_like(dk_acc)
    dv_acc[...] = jnp.zeros_like(dv_acc)

    def block(q_at, o_at, s_at, base, put):
        for c in range(rows // CHUNK):
            low_t = c * CHUNK
            span = slice(low_t, low_t + CHUNK)
            query = q_at[span, :]
            grad = o_at[span, :]
            query_doc = row_docs(
                off_ref, base + low_t + lax.broadcasted_iota(jnp.int32, (1, CHUNK), 1)
            )
            docs = jnp.concatenate([key_doc[...]] * (CHUNK // key_doc.shape[1]), axis=1)
            same = docs == query_doc
            lane_c = lax.broadcasted_iota(jnp.int32, (CHUNK, feats), 1)
            dk_add, dv_add = None, None
            for h in range(heads):
                mine = (lane_c >= h * width) & (lane_c < (h + 1) * width)
                score = contract_last(k_head[h], query)
                prob = jnp.where(same, jnp.exp(score - s_at[h : h + 1, span]), 0.0)
                gp = contract_last(v_head[h], grad)
                ds = (prob * (gp - s_at[heads + h : heads + h + 1, span])).astype(
                    jnp.bfloat16
                )
                query_h = jnp.where(mine, query, jnp.bfloat16(0))
                grad_h = jnp.where(mine, grad, jnp.bfloat16(0))
                dk_h = times(ds, query_h)
                dv_h = times(prob.astype(jnp.bfloat16), grad_h)
                dk_add = dk_h if dk_add is None else dk_add + dk_h
                dv_add = dv_h if dv_add is None else dv_add + dv_h
                put(h, span, times(k_turned[h * width : (h + 1) * width, :], ds))
            dk_acc[...] += dk_add
            dv_acc[...] += dv_add

    def put_own(h, span, value):
        own_dq[h * width : (h + 1) * width, span] = value

    block(q_ref, o_ref, own_s, first, put_own)

    def relay():
        incoming(ahead, 1).wait_recv()
        relay_o().start()

    incoming(direct, 0).wait_recv()
    when_inside(ahead, lambda: relay_q().start())
    when_inside(ahead, relay)

    def visit(i, waits):
        for which in waits:
            incoming(i, which).wait_recv()

        def put(h, span, value):
            part[i, h * width : (h + 1) * width, span] = value.astype(jnp.bfloat16)

        block(slot_q.at[i], slot_o.at[i], slot_s.at[i], (me + offset(i)) * rows, put)
        returning(i, mirror(i)).start()

    def visit_rest(i, _):
        when_inside(i, lambda: visit(i, (0, 1, 2)))
        return 0

    visit(direct, (1, 2))
    when_inside(ahead, lambda: visit(ahead, (0, 2)))
    when_inside(diagonal, lambda: visit(diagonal, (0, 1, 2)))
    when_inside(behind, lambda: visit(behind, (0, 1, 2)))
    lax.fori_loop(4, slots, visit_rest, 0)

    def sharing(which, step, into):
        out = (gq_ref, gk_ref, gv_ref)[which]
        partner = lax.rem(col + step, head_devs)
        column = col if into is None else into
        return pltpu.make_async_remote_copy(
            src_ref=stage.at[which, pl.ds(pl.multiple_of(partner * out_rows, out_rows), out_rows)],
            dst_ref=out.at[:, pl.ds(pl.multiple_of(column * feats, feats), feats)],
            send_sem=out_send.at[which, step - 1],
            recv_sem=out_recv.at[which, step - 1],
            device_id=(me, partner),
            device_id_type=MESH,
        )

    def keeping(which):
        out = (gq_ref, gk_ref, gv_ref)[which]
        return pltpu.make_async_copy(
            stage.at[which, pl.ds(pl.multiple_of(col * out_rows, out_rows), out_rows)],
            out.at[:, pl.ds(pl.multiple_of(col * feats, feats), feats)],
            keep_sem.at[which],
        )

    def share(which):
        for step in range(1, head_devs):
            sharing(which, step, None).start()
        keeping(which).start()

    stage[1] = (dk_acc[...] * scale).astype(jnp.bfloat16)
    stage[2] = dv_acc[...].astype(jnp.bfloat16)
    share(1)
    share(2)

    def gather(i, _):
        @pl.when(inside(i))
        def _():
            returning(i, i).wait_recv()
            own_dq[...] += back[i].astype(jnp.float32)

        return 0

    lax.fori_loop(0, slots, gather, 0)
    stage[0] = own_dq[...].T.astype(jnp.bfloat16)
    share(0)

    def finish(i, _):
        @pl.when(inside(i))
        def _():
            for which in range(3):
                outgoing(i, which).wait_send()
            returning(i, mirror(i)).wait_send()

        return 0

    def finish_diagonal():
        outgoing(diagonal, 2).wait_send()
        returning(diagonal, mirror(diagonal)).wait_send()

    def finish_relay():
        relay_q().wait_send()
        relay_o().wait_send()

    finish(direct, 0)
    when_inside(diagonal, finish_diagonal)
    when_inside(ahead, finish_relay)
    lax.fori_loop(2, slots, finish, 0)
    for which in (1, 2, 0):
        keeping(which).wait()
        for step in range(1, head_devs):
            copy = sharing(which, step, lax.rem(col + head_devs - step, head_devs))
            copy.wait_recv()
            copy.wait_send()


def on_device(seq_count, head_devs, *args):
    queries, log_norm = args[0], args[5]
    rows, feats = queries.shape
    heads = log_norm.shape[0]
    reach = min(8, seq_count // 4)
    slots = 2 * reach
    bf16, f32 = jnp.bfloat16, jnp.float32
    hbm = pl.BlockSpec(memory_space=pltpu.HBM)
    out = jax.ShapeDtypeStruct((rows // head_devs, feats * head_devs), bf16)
    dma = pltpu.SemaphoreType.DMA
    results = pl.pallas_call(
        functools.partial(kernel, reach, seq_count, head_devs, heads),
        out_shape=(out, out, out),
        in_specs=[hbm] * 7,
        out_specs=(hbm,) * 3,
        scratch_shapes=[
            *[pltpu.VMEM((rows, feats), bf16)] * 5,
            pltpu.VMEM(log_norm.shape, f32),
            pltpu.SMEM(args[6].shape, jnp.int32),
            dma((7,)),
            pltpu.VMEM((slots, rows, feats), bf16),
            pltpu.VMEM((slots, rows, feats), bf16),
            pltpu.VMEM((slots, 8, rows), f32),
            pltpu.VMEM((8, rows), f32),
            pltpu.VMEM((feats, rows), f32),
            pltpu.VMEM((slots, feats, rows), bf16),
            pltpu.VMEM((slots, feats, rows), bf16),
            pltpu.VMEM((rows, feats), f32),
            pltpu.VMEM((rows, feats), f32),
            pltpu.VMEM((heads, rows, feats), bf16),
            pltpu.VMEM((heads, rows, feats), bf16),
            pltpu.VMEM((feats, rows), bf16),
            pltpu.VMEM((rows, 128), jnp.int32),
            pltpu.VMEM((3, rows, feats), bf16),
            dma((slots, 3)),
            dma((slots, 3)),
            dma((slots,)),
            dma((slots,)),
            dma((3, head_devs - 1)),
            dma((3, head_devs - 1)),
            dma((3,)),
            dma((2,)),
        ],
        compiler_params=pltpu.CompilerParams(
            collective_id=0, has_side_effects=True
        ),
    )(*args)
    vmem = pl.BlockSpec(memory_space=pltpu.VMEM)
    return pl.pallas_call(
        hand_over,
        out_shape=(out,) * 3,
        in_specs=[vmem] * 3,
        out_specs=(hbm,) * 3,
        scratch_shapes=[dma((3,))],
    )(*results)


def hand_over(*refs):
    sem = refs[6]
    copies = [pltpu.make_async_copy(refs[i], refs[3 + i], sem.at[i]) for i in range(3)]
    for copy in copies:
        copy.start()
    for copy in copies:
        copy.wait()


def solution(mesh):
    seq_count, head_devs = mesh.shape["seq"], mesh.shape["head"]
    in_specs = (
        P("seq", "head"),
        P("seq", "head"),
        P("seq", "head"),
        P("seq", "head"),
        P("seq", "head"),
        P("head", "seq"),
        P(),
    )
    out_specs = (P(("seq", "head"), None),) * 3
    return jax.shard_map(
        functools.partial(on_device, seq_count, head_devs),
        mesh=mesh,
        in_specs=in_specs,
        out_specs=out_specs,
        check_vma=False,
    )
```
